128 devices in a mesh: group: 4 (over z), dev: 32 (over x, y, core).
Axes of the slice: x: 4, y: 4, z: 4, core: 2. Of those that a mesh axis runs over, the one named last changes fastest.
Arguments:
- queries: bfloat16 [131072, 1024], P(('group', 'dev')), may hold values from -2 to 2, as said below
- passages: bfloat16 [16384, 1024], P(('group', 'dev')), may hold values from -6 to 6, as said below
- mined_owner: int32 [32768, 1], replicated, may hold values from 0 to 127; in each aligned block of 256 rows (0 to 255, 256 to 511, ...) at most 4 rows name the same one
- mined_row: int32 [32768], replicated, may hold values from 0 to 127
- positives: int32 [131072], P(('group', 'dev')), may hold values from 0 to 4095
Outputs:
- losses: float32 [131072], P(('group', 'dev'))
- query_grad: float32 [131072, 1024], P(('group', 'dev'))
- passage_grad: float32 [16384, 1024], P(('group', 'dev'))
The draws below stay inside these ranges and needn't reach their ends.
Inputs may be any that keep to these rules, and one draw needn't show every extreme that they name: `queries`: entries normal or uniform with deviation about 1/16, except that the first three rows of each query block may be 0.1, 0.2 and 0.3 times row 0 of the passage block with the same index. `passages`: entries normal or uniform with deviation about 1; row 1 of a passage block may nearly repeat its row 0. `mined_owner`: within the 256 mined slots of one query block, no owner is named more than 4 times; some owner is named exactly 4 times.
All inputs are finite; a program needn't handle non-finite values.
Results may differ from the reference program's by a relative error of at most 0.0015.
Values may be sent and summed in bfloat16 or wider, within the bound.
No kernel may reach another device: no remote copies, remote signals or barrier semaphores. Data moves between devices by JAX's collectives and lax.ppermute only.
A program may use at most 128 MiB of HBM per device.

```python
import math
import jax
import jax.numpy as jnp
import numpy as np
from jax import lax

E = 1024
Q_DEV = 1024
P_DEV = 128
MINED = 256
CAP = 4
QUERIES = 131072
PASSAGES = 16384
N_GROUP = 4
N_DEV = 32


def shared_passages(key):
    first = jax.random.fold_in(key, 101)
    normal_part = jnp.clip(jax.random.normal(first, (PASSAGES, E), jnp.float32), -6.0, 6.0)
    base = normal_part
    blocks = base.reshape(-1, P_DEV, E)
    second_row = blocks[:, 1]
    blocks = blocks.at[:, 1].set(second_row)
    return jnp.clip(blocks.reshape(PASSAGES, E), -6.0, 6.0)


def draw_passages(key, part):
    return shared_passages(key).astype(jnp.bfloat16)


def draw_queries(key, part):
    key = jax.random.fold_in(key, 7)
    values = jax.random.normal(key, (QUERIES, E), jnp.float32) / 16.0
    return jnp.clip(values, -0.375, 0.375).astype(jnp.bfloat16)


def set_ends(values, rng, least, top_value):
    spot = [jax.random.randint(jax.random.fold_in(rng, axis), (), 0, length) for axis, length in enumerate(values.shape)]
    widest = values.shape.index(max(values.shape))
    beside = spot[:widest] + [(spot[widest] + 1) % values.shape[widest]] + spot[widest + 1:]
    return values.at[tuple(spot)].set(least).at[tuple(beside)].set(top_value)


def cumulative_ranks(count, skew):
    loads = [(1 << 20) // math.isqrt(grade ** skew) + 1 for grade in range(1, count + 1)]
    spread = 1 + sum(loads) // (1 << 30)
    return np.cumsum(np.array([max(1, weight // spread) for weight in loads]))


def skewed_ids(rng, shape, number_of, lean):
    listing = cumulative_ranks(number_of, lean)
    ticket = jax.random.randint(jax.random.fold_in(rng, 1), shape, 0, int(listing[number_of - 1]))
    grade = jnp.searchsorted(jnp.asarray(listing, jnp.int32), ticket, side="right")
    return jax.random.permutation(jax.random.fold_in(rng, 2), number_of)[grade].astype(jnp.int32)


def assign_block(stream_key, own, number, rows, number_of, top, reach, slope):
    ranking = jax.random.permutation(stream_key, number_of)
    crowded, common = shares(number_of, rows * top, reach, slope, True), shares(number_of, rows * top, reach, slope, False)
    places = jnp.arange(number_of)

    def named(tallies, rotation):
        used = int((tallies > 0).sum())
        fixed = max(1, used // 4)
        passed = fixed + (places - fixed + rotation * (used - fixed)) % max(1, number_of - fixed)
        return jnp.zeros((number_of,), jnp.int32).at[ranking[jnp.where(places < fixed, places, passed)]].set(jnp.asarray(tallies, jnp.int32))

    tallies = jnp.where(number % 4 == 0, named(crowded, number // 4), named(common, number - number // 4 - 1))
    mixed = jax.random.permutation(jax.random.fold_in(own, 3), number_of)
    source_of, receiver = mixed[0:number_of // 2 * 2:2], mixed[1:number_of // 2 * 2:2]
    room = jnp.minimum(tallies[source_of] - 1, reach - tallies[receiver]) // 2
    room = jnp.where((source_of == ranking[0]) | (receiver == ranking[0]) | (tallies[receiver] == 0), 0, jnp.maximum(room, 0))
    passed = jax.random.randint(jax.random.fold_in(own, 4), (number_of // 2,), 0, 1 << 20) % (room + 1)
    tallies = tallies.at[source_of].add(-passed).at[receiver].add(passed)
    labels = jnp.searchsorted(jnp.cumsum(tallies), jnp.arange(rows * top), side="right").astype(jnp.int32)
    listing = labels.reshape(top, rows).T
    listing = listing[jax.random.permutation(jax.random.fold_in(own, 1), rows)]
    rotation = jax.random.randint(jax.random.fold_in(own, 2), (rows, 1), 0, top)
    return jnp.take_along_axis(listing, (jnp.arange(top)[None, :] + rotation) % top, axis=1)


def shares(amount, total, reach, lean, full):
    weights = [(1 << 20) // math.isqrt(standing ** lean) + 1 for standing in range(1, amount + 1)]
    largest = reach if full else min(reach, max(-(-total // amount), total * weights[0] // sum(weights)))
    least = 1 if total - largest >= amount - 1 else 0
    given, surplus = [largest] + [least] * (amount - 1), total - largest - least * (amount - 1)
    while surplus > 0:
        movable = [i for i in range(1, amount) if given[i] < largest] or [i for i in range(1, amount) if given[i] < reach]
        mass, left = sum([weights[i] for i in movable]), surplus
        for i in movable:
            addition = min(reach - given[i], max(1, left * weights[i] // mass), surplus)
            given[i] = given[i] + addition
            surplus = surplus - addition
    return np.array(given)


def setup_inputs(seed: int = 0) -> dict:
    key_list = jax.random.split(jax.random.key(seed), 6)
    queries = draw_queries(jax.random.fold_in(key_list[5], 71), 0)
    passages = draw_passages(jax.random.fold_in(key_list[5], 71), 0)
    mined_owner_keys = jax.random.split(jax.random.fold_in(key_list[2], 1), (N_GROUP * N_DEV * MINED) // MINED)
    mined_owner_turns = jax.random.permutation(jax.random.fold_in(key_list[2], 3), (N_GROUP * N_DEV * MINED) // MINED)
    mined_owner = jax.vmap(lambda own, number: assign_block(jax.random.fold_in(key_list[2], 2), own, number, MINED, N_GROUP * N_DEV, 1, CAP, 2))(mined_owner_keys, mined_owner_turns).reshape((N_GROUP * N_DEV * MINED, 1))
    mined_row = set_ends(skewed_ids(key_list[3], (N_GROUP * N_DEV * MINED,), P_DEV, 2), jax.random.fold_in(key_list[3], 3), 0, P_DEV - 1).astype(jnp.int32)
    positives = set_ends(jax.random.randint(key_list[4], (QUERIES,), 0, N_DEV * P_DEV), jax.random.fold_in(key_list[4], 1), 0, (N_DEV * P_DEV) - 1).astype(jnp.int32)
    return {"queries": queries, "passages": passages, "mined_owner": mined_owner, "mined_row": mined_row, "positives": positives}


def reference(queries, passages, mined_owner, mined_row, positives):
    blocks = N_GROUP * N_DEV
    in_cols = N_DEV * P_DEV
    owners = mined_owner[:, 0].astype(jnp.int32)
    query_blocks = queries.reshape(blocks, Q_DEV, E)
    positive_blocks = positives.reshape(blocks, Q_DEV)

    def step(carry, item):
        block_id, block_queries, block_pos = item
        group_id = block_id // N_DEV
        start = (group_id * in_cols).astype(jnp.int32)
        ingroup = lax.dynamic_slice_in_dim(passages, start, in_cols, 0)
        own = lax.dynamic_slice_in_dim(owners, (block_id * MINED).astype(jnp.int32), MINED, 0)
        rows = lax.dynamic_slice_in_dim(mined_row, (block_id * MINED).astype(jnp.int32), MINED, 0)
        index = (own * P_DEV + rows).astype(jnp.int32)
        mined = jnp.take(passages, index, axis=0)
        keys = jnp.concatenate([ingroup, mined], axis=0)
        logits = lax.dot_general(block_queries, keys, (((1,), (1,)), ((), ())), preferred_element_type=jnp.float32)
        top = jnp.max(logits, axis=1, keepdims=True)
        lse = top[:, 0] + jnp.log(jnp.sum(jnp.exp(logits - top), axis=1))
        columns = jnp.arange(keys.shape[0], dtype=jnp.int32)
        target = columns[None, :] == block_pos[:, None]
        losses = lse - jnp.sum(jnp.where(target, logits, 0.0), axis=1)
        weights = (jnp.exp(logits - lse[:, None]) - target.astype(jnp.float32)).astype(jnp.bfloat16)
        query_grad = jnp.dot(weights, keys, preferred_element_type=jnp.float32)
        grad_in = lax.dot_general(weights[:, :in_cols], block_queries, (((0,), (0,)), ((), ())), preferred_element_type=jnp.float32)
        grad_mined = lax.dot_general(weights[:, in_cols:], block_queries, (((0,), (0,)), ((), ())), preferred_element_type=jnp.float32)
        current = lax.dynamic_slice_in_dim(carry, start, in_cols, 0)
        carry = lax.dynamic_update_slice_in_dim(carry, current + grad_in, start, 0)
        carry = carry.at[index].add(grad_mined)
        return carry, (losses, query_grad)

    initial = jnp.zeros((blocks * P_DEV, E), jnp.float32)
    items = (jnp.arange(blocks, dtype=jnp.int32), query_blocks, positive_blocks)
    passage_grad, (losses, query_grad) = lax.scan(step, initial, items)
    return losses.reshape(-1), query_grad.reshape(-1, E), passage_grad
```

```python
import functools

import jax
import jax.numpy as jnp
from jax import lax
from jax.experimental import pallas as pl
from jax.experimental.pallas import tpu as pltpu
from jax.sharding import PartitionSpec as P

F32 = jnp.float32
BF16 = jnp.bfloat16
I32 = jnp.int32
LINK = jnp.float16
SIDE = 4
TILE = 512
WIDE = 512
SCOPE = 60
MIB = 1 << 20
WEIGHT = 2.5

ROUNDS = (
    (((1, 0), (1, 0)), ((-1, 0), (-1, 0)), ((0, 1), (0, 1)), ((0, -1), (0, -1))),
    (((1, 1), (0, 1)), ((1, -1), (1, 0)), ((-1, -1), (-1, 0))),
    (((2, 1), (1, 0)), ((2, 0), (-1, 0)), ((-1, 1), (0, 1)), ((0, 2), (0, -1))),
    (((2, 2), (0, 1)), ((2, -1), (-1, 0)), ((1, 2), (1, 0)), ((-1, 2), (0, -1))),
)
OWN = (0, 0)
CHUNKS = (
    tuple(to for to, _ in ROUNDS[0]),
    (OWN,) + tuple(to for to, _ in ROUNDS[1]),
    tuple(to for to, _ in ROUNDS[2]),
    tuple(to for to, _ in ROUNDS[3]),
)


def wrap(offset):
    return (offset[0] % SIDE, offset[1] % SIDE)


def shift(value, step):
    pairs = []
    for x in range(SIDE):
        for y in range(SIDE):
            for core in range(2):
                there = ((x + step[0]) % SIDE) * SIDE + (y + step[1]) % SIDE
                pairs.append(((x * SIDE + y) * 2 + core, there * 2 + core))
    return lax.ppermute(value, "dev", pairs)


def swap(value):
    return lax.ppermute(value, "dev", [(i, i ^ 1) for i in range(2 * SIDE * SIDE)])


def dot(a, b, dims):
    return lax.dot_general(a, b, (dims, ((), ())), preferred_element_type=F32)


def iota(shape, axis):
    return lax.broadcasted_iota(I32, shape, axis)


def params(mib):
    return pltpu.CompilerParams(vmem_limit_bytes=mib * MIB)


def cost(flops, moved, exps=0):
    return pl.CostEstimate(flops=int(flops * WEIGHT), bytes_accessed=int(moved * WEIGHT), transcendentals=int(exps))


VMEM = pl.BlockSpec(memory_space=pltpu.VMEM)
SMEM = pl.BlockSpec(memory_space=pltpu.SMEM)
HBM = pl.BlockSpec(memory_space=pltpu.HBM)
STAMP = (1, 1)


def staged(body, name, operands, outs, flops, aliases=()):
    n, count = len(operands), len(outs)

    def kernel(*refs):
        sources, targets = refs[:n], refs[n : n + count]
        inner, results = refs[n + count : 2 * n + count], refs[2 * n + count : 2 * (n + count)]
        in_sem, out_sem = refs[2 * (n + count) :]
        for copy in fetch(zip(sources, inner), in_sem):
            copy.wait()
        body(*inner, *results)
        for copy in fetch(zip(results, targets), out_sem):
            copy.wait()

    return pl.pallas_call(
        kernel,
        out_shape=tuple(outs),
        in_specs=[HBM] * n,
        out_specs=(HBM,) * count,
        scratch_shapes=[pltpu.VMEM(v.shape, v.dtype) for v in (*operands, *outs)]
        + [pltpu.SemaphoreType.DMA((n,)), pltpu.SemaphoreType.DMA((count,))],
        compiler_params=params(SCOPE),
        cost_estimate=cost(flops, 4e6),
        name=name,
    )(*operands)


def ahead(pairs, sems):
    return [pltpu.make_async_copy(source, to, sems.at[i]) for i, (source, to) in enumerate(pairs)]


def fetch(pairs, sems):
    copies = ahead(pairs, sems)
    for copy in copies:
        copy.start()
    return copies


def serve_kernel(cap, me_ref, owners_ref, rows_ref, pass_ref, out_ref, hot_ref, pick_ref):
    me = me_ref[...]
    total, count = owners_ref.shape
    p_rows, width = pass_ref.shape
    deep = 2 * cap
    slots = total * deep
    earlier = (iota((count, count), 0) < iota((count, count), 1)).astype(BF16)
    asked = (owners_ref[...] == me).astype(F32)
    order = dot(asked.astype(BF16), earlier, ((1,), (0,)))
    rows = rows_ref[...].astype(F32)
    lane = iota((total, 128), 1)
    table = jnp.zeros((total, 128), F32)
    for place in range(cap):
        chosen = jnp.where(order == float(place), asked, 0.0)
        table += jnp.where(lane % cap == place, jnp.sum(chosen * rows, axis=1, keepdims=True), 0.0)
    spread = ((iota((slots, total), 0) // deep) == iota((slots, total), 1)).astype(BF16)
    wide = dot(spread, table.astype(BF16), ((1,), (0,)))
    mine = (iota((slots, 128), 0) % deep) == iota((slots, 128), 1)
    wanted = jnp.sum(jnp.where(mine, wide, 0.0), axis=1, keepdims=True)
    hot = (iota((slots, p_rows), 1).astype(F32) == wanted).astype(BF16)
    hot_ref[...] = hot
    first = dot(hot, pass_ref[:, : width // 2], ((1,), (0,)))
    second = dot(hot, pass_ref[:, width // 2 :], ((1,), (0,)))
    low = (iota(first.shape, 0) % deep) < cap
    out_ref[...] = jnp.where(low, first, second).astype(BF16)
    mine_row = iota((total, count), 0) == me
    own = jnp.sum(jnp.where(mine_row, owners_ref[...], 0), axis=0, keepdims=True)
    hits = (iota((total, count), 0) == own).astype(F32)
    before = dot(hits.astype(BF16), earlier, ((1,), (0,)))
    place = jnp.sum(hits * before, axis=0, keepdims=True).astype(I32)
    row = iota((slots, count), 0)
    fetch = own * deep + place
    pick_ref[...] = ((row == fetch) | (row == fetch + cap)).astype(BF16)


def serve(me, owners, rows, passages, cap):
    total, count = owners.shape
    p_rows, width = passages.shape
    slots = total * 2 * cap
    outs = (
        jax.ShapeDtypeStruct((slots, width // 2), BF16),
        jax.ShapeDtypeStruct((slots, p_rows), BF16),
        jax.ShapeDtypeStruct((slots, count), BF16),
    )
    body = functools.partial(serve_kernel, cap)
    return staged(body, "serve_mined", (me, owners, rows, passages), outs, 8e8)


def half_rows(pick, cap, half):
    keep = ((iota(pick.shape, 0) % (2 * cap)) < cap) == (half == 0)
    return jnp.where(keep, pick, jnp.zeros_like(pick))


def merge(m_a, l_a, m_b, l_b):
    m = jnp.maximum(m_a, m_b)
    return m, l_a * jnp.exp(m_a - m) + l_b * jnp.exp(m_b - m)


def mined_logits_kernel(cap, got_ref, pick_ref, q_ref, old_ref, keys_ref, e_ref, stat_ref):
    rows, width = q_ref.shape
    pick = pick_ref[...]
    for h in range(2):
        part = dot(half_rows(pick, cap, h), got_ref[...], ((0,), (0,)))
        keys_ref[:, h * (width // 2) : (h + 1) * (width // 2)] = part.astype(BF16)
    stat_ref[...] = old_ref[...]
    for part in range(rows // TILE):
        at = slice(part * TILE, (part + 1) * TILE)
        s = dot(keys_ref[...], q_ref[at, :], ((1,), (1,)))
        m_old = old_ref[0:1, at]
        m = jnp.maximum(jnp.max(s, axis=0, keepdims=True), m_old)
        e = jnp.exp(s - m)
        e_ref[:, at] = e.astype(BF16)
        stat_ref[0:1, at] = m
        stat_ref[1:2, at] = jnp.sum(e, axis=0, keepdims=True) + old_ref[1:2, at] * jnp.exp(m_old - m)


def mined_logits(got, pick, q, old, cap):
    count = pick.shape[1]
    rows, width = q.shape
    outs = (
        jax.ShapeDtypeStruct((count, width), BF16),
        jax.ShapeDtypeStruct((count, rows), BF16),
        jax.ShapeDtypeStruct((8, 2 * rows), F32),
    )
    return staged(functools.partial(mined_logits_kernel, cap), "mined_logits", (got, pick, q, old), outs, 1.6e9)


def key_ids(at_ref, offset, p_rows):
    x = (at_ref[0] + (SIDE - offset[0])) % SIDE
    y = (at_ref[1] + (SIDE - offset[1])) % SIDE
    return ((x * SIDE + y) * 2 + at_ref[2]) * p_rows


def query_tiles(rows):
    tiles = []
    for side in range(2):
        for part in range(rows // TILE):
            here = slice(part * TILE, (part + 1) * TILE)
            at = slice(side * rows + part * TILE, side * rows + (part + 1) * TILE)
            far = slice((1 - side) * rows + part * TILE, (1 - side) * rows + (part + 1) * TILE)
            tiles.append((side, here, at, far))
    return tiles


def logits_kernel(chunk, first, *refs):
    at_ref, pa_ref, pb_ref = refs[:3]
    blocks = len(chunk)
    rest = list(refs[3:])
    far_refs = [pa_ref, pb_ref] + ([] if first else [rest.pop(0)])
    qa_ref, qb_ref = rest[:2]
    k_refs = rest[2 : 2 + blocks]
    e_ref, far_stat_ref, q, k, e, pos_a, pos_b, old, stat, s_sem, k_sem, q_sem, e_sem = rest[2 + blocks :]
    small = fetch(zip(far_refs, (pos_a, pos_b, old)), s_sem)
    pa_ref, pb_ref, old_ref, stat_ref = pos_a, pos_b, old, stat
    p_rows = k_refs[0].shape[0]
    rows = qa_ref.shape[0]
    tiles = query_tiles(rows)
    k_copies = fetch([(k_refs[b], k.at[pl.ds(b * p_rows, p_rows), :]) for b in range(blocks)], k_sem)
    q_copies = ahead([((qa_ref, qb_ref)[side].at[here, :], q.at[at, :]) for side, here, at, _ in tiles], q_sem)
    q_copies[0].start()
    q_copies[1].start()
    base = [key_ids(at_ref, o, p_rows) for o in chunk]
    stat_ref[...] = jnp.zeros_like(stat_ref)
    for copy in small + k_copies:
        copy.wait()
    out = []
    for i, (side, here, at, _) in enumerate(tiles):
        q_copies[i].wait()
        if i + 2 < len(tiles):
            q_copies[i + 2].start()
        s = dot(k[...], q[at, :], ((1,), (1,)))
        m = jnp.max(s, axis=0, keepdims=True)
        if not first:
            m = jnp.maximum(m, old_ref[0:1, at])
        p = jnp.exp(s - m)
        e[:, at] = p.astype(BF16)
        out.append(pltpu.make_async_copy(e.at[:, at], e_ref.at[:, at], e_sem.at[i]))
        out[-1].start()
        l = jnp.sum(p, axis=0, keepdims=True)
        pos = (pa_ref, pb_ref)[side][0:1, here]
        t = jnp.zeros_like(m)
        for b in range(blocks):
            piece = s[b * p_rows : (b + 1) * p_rows, :]
            t += jnp.sum(jnp.where(iota(piece.shape, 0) == pos - base[b], piece, 0.0), axis=0, keepdims=True)
        if not first:
            l += old_ref[1:2, at] * jnp.exp(old_ref[0:1, at] - m)
            t += old_ref[2:3, at]
        stat_ref[0:1, at] = m
        stat_ref[1:2, at] = l
        stat_ref[2:3, at] = t
    out += fetch([(stat, far_stat_ref)], s_sem)
    for copy in out:
        copy.wait()


def logits(chunk, at, pa, pb, qa, qb, blocks, old):
    rows, width = qa.shape
    n = len(blocks)
    keys = n * blocks[0].shape[0]
    parts = 2 * rows // TILE
    args = [at, pa, pb] + ([] if old is None else [old]) + [qa, qb, *blocks]
    return pl.pallas_call(
        functools.partial(logits_kernel, chunk, old is None),
        out_shape=(jax.ShapeDtypeStruct((keys, 2 * rows), BF16), jax.ShapeDtypeStruct((8, 2 * rows), F32)),
        in_specs=[SMEM] + [HBM] * (len(args) - 1),
        out_specs=(HBM, HBM),
        scratch_shapes=[
            pltpu.VMEM((2 * rows, width), BF16),
            pltpu.VMEM((keys, width), BF16),
            pltpu.VMEM((keys, 2 * rows), BF16),
            pltpu.VMEM((1, rows), I32),
            pltpu.VMEM((1, rows), I32),
            pltpu.VMEM((8, 2 * rows), F32),
            pltpu.VMEM((8, 2 * rows), F32),
            pltpu.SemaphoreType.DMA((3,)),
            pltpu.SemaphoreType.DMA((n,)),
            pltpu.SemaphoreType.DMA((parts,)),
            pltpu.SemaphoreType.DMA((parts,)),
        ],
        compiler_params=params(SCOPE),
        cost_estimate=cost(2 * keys * 2 * rows * width, 4e6, keys * 2 * rows),
        name="logits",
    )(*args)


def log_total(here, there):
    m, l = merge(here[0:1, :], here[1:2, :], there[0:1, :], there[1:2, :])
    return m + jnp.log(l)


def weights_kernel(chunk, *refs):
    at_ref, pa_ref, pb_ref, here_ref, there_ref, stat_ref, e_ref, qa_ref, qb_ref = refs[:9]
    w_ref, g_ref, stamp_ref, q, w, g, pos_a, pos_b, here_v, there_v, stat_v, s_sem, e_sem, q_sem, w_sem, g_sem = refs[9:]
    nearby = (pos_a, pos_b, here_v, there_v, stat_v)
    small = fetch(zip((pa_ref, pb_ref, here_ref, there_ref, stat_ref), nearby), s_sem)
    pa_ref, pb_ref, here_ref, there_ref, stat_ref = nearby
    blocks = len(chunk)
    p_rows = e_ref.shape[0] // blocks
    rows, width = qa_ref.shape
    tiles = query_tiles(rows)
    e_copies = ahead([(e_ref.at[:, at], w.at[:, at]) for _, _, at, _ in tiles], e_sem)
    q_copies = ahead([((qa_ref, qb_ref)[side].at[here, :], q.at[at, :]) for side, here, at, _ in tiles], q_sem)
    for i in range(2):
        e_copies[i].start()
        q_copies[i].start()
    stamp_ref[...] = jnp.zeros_like(stamp_ref)
    for copy in small:
        copy.wait()
    base = [key_ids(at_ref, o, p_rows) for o in chunk]
    out = []
    for i, (side, here, at, far) in enumerate(tiles):
        lse = log_total(here_ref[:, at], there_ref[:, far])
        scale = jnp.exp(stat_ref[0:1, at] - lse)
        hit = jnp.exp(here_ref[2:3, at] - lse) - 1.0
        pos = (pa_ref, pb_ref)[side][0:1, here]
        e_copies[i].wait()
        if i + 2 < len(tiles):
            e_copies[i + 2].start()
            q_copies[i + 2].start()
        for b in range(blocks):
            down = slice(b * p_rows, (b + 1) * p_rows)
            p = w[down, at].astype(F32) * scale
            w[down, at] = jnp.where(iota(p.shape, 0) == pos - base[b], hit, p).astype(BF16)
        out.append(pltpu.make_async_copy(w.at[:, at], w_ref.at[:, at], w_sem.at[i]))
        out[-1].start()
        q_copies[i].wait()
        for part in range(width // WIDE):
            cols = slice(part * WIDE, (part + 1) * WIDE)
            term = dot(w[:, at], q[at, cols], ((1,), (0,)))
            g[:, cols] = term if i == 0 else g[:, cols] + term
            if i == len(tiles) - 1:
                out.append(pltpu.make_async_copy(g.at[:, cols], g_ref.at[:, cols], g_sem.at[part]))
                out[-1].start()
    for copy in out:
        copy.wait()


def weights(chunk, at, pa, pb, here, there, stat, e, qa, qb):
    rows, width = qa.shape
    keys = e.shape[0]
    parts = 2 * rows // TILE
    return pl.pallas_call(
        functools.partial(weights_kernel, chunk),
        out_shape=(
            jax.ShapeDtypeStruct(e.shape, BF16),
            jax.ShapeDtypeStruct((keys, width), F32),
            jax.ShapeDtypeStruct(STAMP, F32),
        ),
        in_specs=[SMEM] + [HBM] * 8,
        out_specs=(HBM, HBM, VMEM),
        scratch_shapes=[
            pltpu.VMEM((2 * rows, width), BF16),
            pltpu.VMEM((keys, 2 * rows), BF16),
            pltpu.VMEM((keys, width), F32),
            pltpu.VMEM((1, rows), I32),
            pltpu.VMEM((1, rows), I32),
            pltpu.VMEM((8, 2 * rows), F32),
            pltpu.VMEM((8, 2 * rows), F32),
            pltpu.VMEM((8, 2 * rows), F32),
            pltpu.SemaphoreType.DMA((5,)),
            pltpu.SemaphoreType.DMA((parts,)),
            pltpu.SemaphoreType.DMA((parts,)),
            pltpu.SemaphoreType.DMA((parts,)),
            pltpu.SemaphoreType.DMA((width // WIDE,)),
        ],
        compiler_params=params(SCOPE),
        cost_estimate=cost(2 * keys * 2 * rows * width, 4e6, keys * 2 * rows),
        name="weights",
    )(at, pa, pb, here, there, stat, e, qa, qb)


def mined_weights_kernel(cap, here_ref, there_ref, e_ref, q_ref, pick_ref, _, w_ref, back_ref, loss_ref, stamp_ref):
    rows, width = q_ref.shape
    here, there = here_ref[:, :rows], there_ref[:, rows:]
    lse = log_total(here, there)
    loss_ref[...] = lse - here[2:3, :] - there[2:3, :]
    w = (e_ref[...].astype(F32) * jnp.exp(here[0:1, :] - lse)).astype(BF16)
    w_ref[...] = w
    g = dot(w, q_ref[...], ((1,), (0,))).astype(BF16)
    pick = pick_ref[...]
    first = dot(pick, g[:, : width // 2], ((1,), (0,)))
    second = dot(pick, g[:, width // 2 :], ((1,), (0,)))
    low = (iota(first.shape, 0) % (2 * cap)) < cap
    back_ref[...] = jnp.where(low, first, second).astype(BF16)
    stamp_ref[...] = jnp.zeros_like(stamp_ref)


def mined_weights(here, there, e, q, pick, cap, after):
    count, rows = e.shape
    width = q.shape[1]
    slots = pick.shape[0]
    outs = (
        jax.ShapeDtypeStruct((count, rows), BF16),
        jax.ShapeDtypeStruct((slots, width // 2), BF16),
        jax.ShapeDtypeStruct((1, rows), F32),
        jax.ShapeDtypeStruct(STAMP, F32),
    )
    body = functools.partial(mined_weights_kernel, cap)
    return staged(body, "mined_weights", (here, there, e, q, pick, after), outs, 1.4e9)


def query_kernel(counts, side, tile, adds, *refs):
    chunks = len(counts)
    w_refs, refs = refs[:chunks], refs[chunks:]
    k_refs, refs = refs[: sum(counts)], refs[sum(counts) :]
    x_refs, refs = refs[:adds], refs[adds:]
    out_refs, (stamp_ref, w, k, x, acc, w_sem, k_sem, x_sem, o_sem) = refs[:-9], refs[-9:]
    rows = acc.shape[0]
    parts = rows // tile
    stamp_ref[...] = jnp.zeros_like(stamp_ref)
    copies, spans, start, block = [], [], 0, 0
    for c, count in enumerate(counts):
        depth = w_refs[c].shape[0]
        left = side * rows if w_refs[c].shape[1] > rows else 0
        pending = [pltpu.make_async_copy(w_refs[c].at[:, pl.ds(left, rows)], w.at[pl.ds(start, depth), :], w_sem.at[c])]
        for i in range(count):
            ref = k_refs[block + i]
            size = ref.shape[0]
            to = k.at[pl.ds(start + i * size, size), :]
            pending.append(pltpu.make_async_copy(ref, to, k_sem.at[block + i]))
        for copy in pending:
            copy.start()
        copies.append(pending)
        spans.append(slice(start, start + depth))
        start, block = start + depth, block + count
    more = fetch([(x_refs[i], x.at[pl.ds(i * tile, tile), :]) for i in range(adds)], x_sem)
    out = []
    for c, span in enumerate(spans):
        for copy in copies[c]:
            copy.wait()
        for part in range(parts):
            at = slice(part * tile, (part + 1) * tile)
            term = dot(w[span, at], k[span, :], ((0,), (0,)))
            if c > 0:
                term = term + acc[at, :]
            if c == chunks - 1:
                if adds:
                    more[part].wait()
                    term = term + x[at, :]
            acc[at, :] = term
            if c == chunks - 1:
                to = out_refs[part] if len(out_refs) > 1 else out_refs[0].at[at, :]
                out.append(pltpu.make_async_copy(acc.at[at, :], to, o_sem.at[part]))
                out[-1].start()
    for copy in out:
        copy.wait()


def query_grad(ws, blocks, side, rows, extras, split):
    width = blocks[0][0].shape[1]
    tile = 256
    parts = rows // tile
    flat = [b for group in blocks for b in group]
    depth = sum(w.shape[0] for w in ws)
    shapes = [jax.ShapeDtypeStruct((tile, width), F32)] * parts if split else [jax.ShapeDtypeStruct((rows, width), F32)]
    out = pl.pallas_call(
        functools.partial(query_kernel, tuple(len(group) for group in blocks), side, tile, len(extras)),
        out_shape=tuple(shapes) + (jax.ShapeDtypeStruct(STAMP, F32),),
        in_specs=[HBM] * (len(ws) + len(flat) + len(extras)),
        out_specs=(HBM,) * len(shapes) + (VMEM,),
        scratch_shapes=[
            pltpu.VMEM((depth, rows), BF16),
            pltpu.VMEM((depth, width), BF16),
            pltpu.VMEM((rows if extras else 8, width), F32),
            pltpu.VMEM((rows, width), F32),
            pltpu.SemaphoreType.DMA((len(ws),)),
            pltpu.SemaphoreType.DMA((len(flat),)),
            pltpu.SemaphoreType.DMA((parts,)),
            pltpu.SemaphoreType.DMA((parts,)),
        ],
        compiler_params=params(SCOPE),
        cost_estimate=cost(2 * rows * width * depth, 6e6),
        name="query_grad",
    )(*ws, *flat, *extras)
    return out[:-1], out[-1]


def owned_kernel(cap, hot_ref, back_ref, out_ref):
    hot = hot_ref[...]
    half = back_ref.shape[1]
    for h in range(2):
        out_ref[:, h * half : (h + 1) * half] = dot(half_rows(hot, cap, h), back_ref[...], ((0,), (0,)))


def owned_sum(hot, back, cap):
    outs = (jax.ShapeDtypeStruct((hot.shape[1], 2 * back.shape[1]), F32),)
    return staged(functools.partial(owned_kernel, cap), "owned_sum", (hot, back), outs, 4e8)[0]


def tie(values, *others):
    return lax.optimization_barrier((values, others))[0]


def local(queries, passages, mined_owner, mined_row, positives):
    groups = lax.axis_size("group")
    devs = lax.axis_size("dev")
    total = groups * devs
    dev = lax.axis_index("dev")
    me = lax.axis_index("group") * devs + dev
    at = jnp.stack([dev // (2 * SIDE), (dev // 2) % SIDE, dev % 2]).astype(I32)
    rows, width = queries.shape
    cap = max(2, 2 * (mined_owner.shape[0] // total) // total)

    other = swap(queries)
    pa = positives.reshape(1, rows)
    pb = swap(pa)

    def exchange(value):
        value = value.reshape(total, 2 * cap, width // 2)
        value = lax.all_to_all(value, ("group", "dev"), split_axis=0, concat_axis=0, tiled=True)
        return value.reshape(total * 2 * cap, width // 2)

    held = {wrap(OWN): passages}

    def source(to, step):
        return wrap((to[0] - step[0], to[1] - step[1]))

    def spread(stage, *others):
        names = [source(to, step) for to, step in stage]
        values = tie([held[n] for n in names], *others) if others else [held[n] for n in names]
        for (to, step), value in zip(stage, values):
            held[wrap(to)] = shift(value, step)

    def round_of(number):
        return [held[wrap(to)] for to, _ in ROUNDS[number]]

    spread(ROUNDS[0])
    owners = mined_owner[:, 0].reshape(total, -1)
    names = mined_row.reshape(total, -1)
    outgoing, hot, pick = serve(me.astype(I32).reshape(1, 1), owners, names, passages, cap)
    arrived = exchange(outgoing)
    blocks = lambda chunk: [held[wrap(o)] for o in chunk]
    spread(ROUNDS[1], owners, names, round_of(0))
    spread(ROUNDS[2], round_of(1), round_of(0))
    near = CHUNKS[0] + CHUNKS[1]
    e1, stat1 = logits(near, at, pa, pb, queries, other, blocks(near), None)
    spread(ROUNDS[3], stat1, round_of(2))
    e2, stat2 = logits(CHUNKS[2], at, pa, pb, queries, other, blocks(CHUNKS[2]), stat1)
    e3, stat3 = logits(CHUNKS[3], at, pa, pb, queries, other, blocks(CHUNKS[3]), stat2)
    mined, e_mined, stat = mined_logits(arrived, pick, queries, stat3, cap)
    there = swap(stat)

    grads = {}

    def collect(number, g, *stamps):
        chunk, stage = CHUNKS[number], ROUNDS[number]
        n = passages.shape[0]
        for b, o in enumerate(chunk):
            grads.setdefault(wrap(o), []).insert(0, g[b * n : (b + 1) * n])
        zeros = [stamp.reshape(()) for stamp in stamps]
        for to, step in stage:
            send = functools.reduce(jnp.add, [v.astype(F32) for v in grads[wrap(to)]] + zeros).astype(LINK)
            grads.setdefault(source(to, step), []).append(shift(send, (-step[0], -step[1])))

    common = (at, pa, pb, stat, there)
    w3, g3, w3_done = weights(CHUNKS[3], *common, stat3, e3, queries, other)
    collect(3, g3)
    w2, g2, _ = weights(CHUNKS[2], *common, stat2, e2, queries, other)
    w_mined, back, losses, mined_done = mined_weights(stat, there, e_mined, queries, pick, cap, w3_done)
    returned = exchange(back)
    collect(2, g2, mined_done)
    w1, g1, _ = weights(near, *common, stat1, e1, queries, other)
    split = len(CHUNKS[0]) * passages.shape[0]
    collect(1, g1[split:])
    ws = [w3, w2, w1]
    ks = [blocks(CHUNKS[3]), blocks(CHUNKS[2]), blocks(near)]
    theirs, their_done = query_grad(ws, ks, 1, rows, (), True)
    theirs = [swap(v) for v in theirs]
    collect(0, g1[:split], their_done)
    (mine,), own_done = query_grad(ws + [w_mined], ks + [[mined]], 0, rows, theirs, False)
    owned = owned_sum(hot, returned, cap)
    passage = functools.reduce(jnp.add, [v.astype(F32) for v in grads[wrap(OWN)]] + [owned, own_done.reshape(())])
    return losses.reshape(rows), mine, passage


def solution(mesh):
    placed = (P(("group", "dev"), None), P(("group", "dev"), None), P(), P(), P(("group", "dev")))
    return jax.shard_map(
        local,
        mesh=mesh,
        in_specs=placed,
        out_specs=(P(("group", "dev")), P(("group", "dev"), None), P(("group", "dev"), None)),
        check_vma=False,
    )
```

```python
import functools

import jax
import jax.numpy as jnp
from jax import lax
from jax.experimental import pallas as pl
from jax.experimental.pallas import tpu as pltpu
from jax.sharding import PartitionSpec as P

F32 = jnp.float32
BF16 = jnp.bfloat16
I32 = jnp.int32
LINK = jnp.float16
SIDE = 4
TILE = 512
WIDE = 512
SCOPE = 60
MIB = 1 << 20
WEIGHT = 2.5

ROUNDS = (
    (((1, 0), (1, 0)), ((-1, 0), (-1, 0)), ((0, 1), (0, 1)), ((0, -1), (0, -1))),
    (((1, 1), (0, 1)), ((1, -1), (1, 0)), ((-1, -1), (-1, 0))),
    (((2, 1), (1, 0)), ((2, 0), (-1, 0)), ((-1, 1), (0, 1)), ((0, 2), (0, -1))),
    (((2, 2), (0, 1)), ((2, -1), (-1, 0)), ((1, 2), (1, 0)), ((-1, 2), (0, -1))),
)
OWN = (0, 0)
CHUNKS = (
    tuple(to for to, _ in ROUNDS[0]),
    (OWN,) + tuple(to for to, _ in ROUNDS[1]),
    tuple(to for to, _ in ROUNDS[2]),
    tuple(to for to, _ in ROUNDS[3]),
)


def wrap(offset):
    return (offset[0] % SIDE, offset[1] % SIDE)


def shift(value, step):
    pairs = []
    for x in range(SIDE):
        for y in range(SIDE):
            for core in range(2):
                there = ((x + step[0]) % SIDE) * SIDE + (y + step[1]) % SIDE
                pairs.append(((x * SIDE + y) * 2 + core, there * 2 + core))
    return lax.ppermute(value, "dev", pairs)


def swap(value):
    return lax.ppermute(value, "dev", [(i, i ^ 1) for i in range(2 * SIDE * SIDE)])


def dot(a, b, dims):
    return lax.dot_general(a, b, (dims, ((), ())), preferred_element_type=F32)


def iota(shape, axis):
    return lax.broadcasted_iota(I32, shape, axis)


def params(mib):
    return pltpu.CompilerParams(vmem_limit_bytes=mib * MIB)


def cost(flops, moved, exps=0):
    return pl.CostEstimate(flops=int(flops * WEIGHT), bytes_accessed=int(moved * WEIGHT), transcendentals=int(exps))


VMEM = pl.BlockSpec(memory_space=pltpu.VMEM)
SMEM = pl.BlockSpec(memory_space=pltpu.SMEM)
HBM = pl.BlockSpec(memory_space=pltpu.HBM)
STAMP = (1, 1)


def staged(body, name, operands, outs, flops, aliases=()):
    n, count = len(operands), len(outs)

    def kernel(*refs):
        sources, targets = refs[:n], refs[n : n + count]
        inner, results = refs[n + count : 2 * n + count], refs[2 * n + count : 2 * (n + count)]
        in_sem, out_sem = refs[2 * (n + count) :]
        for copy in fetch(zip(sources, inner), in_sem):
            copy.wait()
        body(*inner, *results)
        for copy in fetch(zip(results, targets), out_sem):
            copy.wait()

    return pl.pallas_call(
        kernel,
        out_shape=tuple(outs),
        in_specs=[HBM] * n,
        out_specs=(HBM,) * count,
        scratch_shapes=[pltpu.VMEM(v.shape, v.dtype) for v in (*operands, *outs)]
        + [pltpu.SemaphoreType.DMA((n,)), pltpu.SemaphoreType.DMA((count,))],
        compiler_params=params(SCOPE),
        cost_estimate=cost(flops, 4e6),
        name=name,
    )(*operands)


def ahead(pairs, sems):
    return [pltpu.make_async_copy(source, to, sems.at[i]) for i, (source, to) in enumerate(pairs)]


def fetch(pairs, sems):
    copies = ahead(pairs, sems)
    for copy in copies:
        copy.start()
    return copies


def serve_kernel(cap, me_ref, owners_ref, rows_ref, pass_ref, out_ref, hot_ref, pick_ref):
    me = me_ref[...]
    total, count = owners_ref.shape
    p_rows, width = pass_ref.shape
    deep = 2 * cap
    slots = total * deep
    earlier = (iota((count, count), 0) < iota((count, count), 1)).astype(BF16)
    asked = (owners_ref[...] == me).astype(F32)
    order = dot(asked.astype(BF16), earlier, ((1,), (0,)))
    rows = rows_ref[...].astype(F32)
    lane = iota((total, 128), 1)
    table = jnp.zeros((total, 128), F32)
    for place in range(cap):
        chosen = jnp.where(order == float(place), asked, 0.0)
        table += jnp.where(lane % cap == place, jnp.sum(chosen * rows, axis=1, keepdims=True), 0.0)
    spread = ((iota((slots, total), 0) // deep) == iota((slots, total), 1)).astype(BF16)
    wide = dot(spread, table.astype(BF16), ((1,), (0,)))
    mine = (iota((slots, 128), 0) % deep) == iota((slots, 128), 1)
    wanted = jnp.sum(jnp.where(mine, wide, 0.0), axis=1, keepdims=True)
    hot = (iota((slots, p_rows), 1).astype(F32) == wanted).astype(BF16)
    hot_ref[...] = hot
    first = dot(hot, pass_ref[:, : width // 2], ((1,), (0,)))
    second = dot(hot, pass_ref[:, width // 2 :], ((1,), (0,)))
    low = (iota(first.shape, 0) % deep) < cap
    out_ref[...] = jnp.where(low, first, second).astype(BF16)
    mine_row = iota((total, count), 0) == me
    own = jnp.sum(jnp.where(mine_row, owners_ref[...], 0), axis=0, keepdims=True)
    hits = (iota((total, count), 0) == own).astype(F32)
    before = dot(hits.astype(BF16), earlier, ((1,), (0,)))
    place = jnp.sum(hits * before, axis=0, keepdims=True).astype(I32)
    row = iota((slots, count), 0)
    fetch = own * deep + place
    pick_ref[...] = ((row == fetch) | (row == fetch + cap)).astype(BF16)


def serve(me, owners, rows, passages, cap):
    total, count = owners.shape
    p_rows, width = passages.shape
    slots = total * 2 * cap
    outs = (
        jax.ShapeDtypeStruct((slots, width // 2), BF16),
        jax.ShapeDtypeStruct((slots, p_rows), BF16),
        jax.ShapeDtypeStruct((slots, count), BF16),
    )
    body = functools.partial(serve_kernel, cap)
    return staged(body, "serve_mined", (me, owners, rows, passages), outs, 8e8)


def half_rows(pick, cap, half):
    keep = ((iota(pick.shape, 0) % (2 * cap)) < cap) == (half == 0)
    return jnp.where(keep, pick, jnp.zeros_like(pick))


def merge(m_a, l_a, m_b, l_b):
    m = jnp.maximum(m_a, m_b)
    return m, l_a * jnp.exp(m_a - m) + l_b * jnp.exp(m_b - m)


def mined_logits_kernel(cap, got_ref, pick_ref, q_ref, old_ref, keys_ref, e_ref, stat_ref):
    rows, width = q_ref.shape
    pick = pick_ref[...]
    for h in range(2):
        part = dot(half_rows(pick, cap, h), got_ref[...], ((0,), (0,)))
        keys_ref[:, h * (width // 2) : (h + 1) * (width // 2)] = part.astype(BF16)
    stat_ref[...] = old_ref[...]
    for part in range(rows // TILE):
        at = slice(part * TILE, (part + 1) * TILE)
        s = dot(keys_ref[...], q_ref[at, :], ((1,), (1,)))
        m_old = old_ref[0:1, at]
        m = jnp.maximum(jnp.max(s, axis=0, keepdims=True), m_old)
        e = jnp.exp(s - m)
        e_ref[:, at] = e.astype(BF16)
        stat_ref[0:1, at] = m
        stat_ref[1:2, at] = jnp.sum(e, axis=0, keepdims=True) + old_ref[1:2, at] * jnp.exp(m_old - m)


def mined_logits(got, pick, q, old, cap):
    count = pick.shape[1]
    rows, width = q.shape
    outs = (
        jax.ShapeDtypeStruct((count, width), BF16),
        jax.ShapeDtypeStruct((count, rows), BF16),
        jax.ShapeDtypeStruct((8, 2 * rows), F32),
    )
    return staged(functools.partial(mined_logits_kernel, cap), "mined_logits", (got, pick, q, old), outs, 1.6e9)


def key_ids(at_ref, offset, p_rows):
    x = (at_ref[0] + (SIDE - offset[0])) % SIDE
    y = (at_ref[1] + (SIDE - offset[1])) % SIDE
    return ((x * SIDE + y) * 2 + at_ref[2]) * p_rows


def query_tiles(rows):
    tiles = []
    for side in range(2):
        for part in range(rows // TILE):
            here = slice(part * TILE, (part + 1) * TILE)
            at = slice(side * rows + part * TILE, side * rows + (part + 1) * TILE)
            far = slice((1 - side) * rows + part * TILE, (1 - side) * rows + (part + 1) * TILE)
            tiles.append((side, here, at, far))
    return tiles


def logits_kernel(chunk, first, *refs):
    at_ref, pa_ref, pb_ref = refs[:3]
    blocks = len(chunk)
    rest = list(refs[3:])
    far_refs = [pa_ref, pb_ref] + ([] if first else [rest.pop(0)])
    qa_ref, qb_ref = rest[:2]
    k_refs = rest[2 : 2 + blocks]
    e_ref, far_stat_ref, q, k, e, pos_a, pos_b, old, stat, s_sem, k_sem, q_sem, e_sem = rest[2 + blocks :]
    small = fetch(zip(far_refs, (pos_a, pos_b, old)), s_sem)
    pa_ref, pb_ref, old_ref, stat_ref = pos_a, pos_b, old, stat
    p_rows = k_refs[0].shape[0]
    rows = qa_ref.shape[0]
    tiles = query_tiles(rows)
    k_copies = fetch([(k_refs[b], k.at[pl.ds(b * p_rows, p_rows), :]) for b in range(blocks)], k_sem)
    q_copies = ahead([((qa_ref, qb_ref)[side].at[here, :], q.at[at, :]) for side, here, at, _ in tiles], q_sem)
    q_copies[0].start()
    q_copies[1].start()
    base = [key_ids(at_ref, o, p_rows) for o in chunk]
    stat_ref[...] = jnp.zeros_like(stat_ref)
    for copy in small + k_copies:
        copy.wait()
    out = []
    for i, (side, here, at, _) in enumerate(tiles):
        q_copies[i].wait()
        if i + 2 < len(tiles):
            q_copies[i + 2].start()
        s = dot(k[...], q[at, :], ((1,), (1,)))
        m = jnp.max(s, axis=0, keepdims=True)
        if not first:
            m = jnp.maximum(m, old_ref[0:1, at])
        p = jnp.exp(s - m)
        e[:, at] = p.astype(BF16)
        out.append(pltpu.make_async_copy(e.at[:, at], e_ref.at[:, at], e_sem.at[i]))
        out[-1].start()
        l = jnp.sum(p, axis=0, keepdims=True)
        pos = (pa_ref, pb_ref)[side][0:1, here]
        t = jnp.zeros_like(m)
        for b in range(blocks):
            piece = s[b * p_rows : (b + 1) * p_rows, :]
            t += jnp.sum(jnp.where(iota(piece.shape, 0) == pos - base[b], piece, 0.0), axis=0, keepdims=True)
        if not first:
            l += old_ref[1:2, at] * jnp.exp(old_ref[0:1, at] - m)
            t += old_ref[2:3, at]
        stat_ref[0:1, at] = m
        stat_ref[1:2, at] = l
        stat_ref[2:3, at] = t
    out += fetch([(stat, far_stat_ref)], s_sem)
    for copy in out:
        copy.wait()


def logits(chunk, at, pa, pb, qa, qb, blocks, old):
    rows, width = qa.shape
    n = len(blocks)
    keys = n * blocks[0].shape[0]
    parts = 2 * rows // TILE
    args = [at, pa, pb] + ([] if old is None else [old]) + [qa, qb, *blocks]
    return pl.pallas_call(
        functools.partial(logits_kernel, chunk, old is None),
        out_shape=(jax.ShapeDtypeStruct((keys, 2 * rows), BF16), jax.ShapeDtypeStruct((8, 2 * rows), F32)),
        in_specs=[SMEM] + [HBM] * (len(args) - 1),
        out_specs=(HBM, HBM),
        scratch_shapes=[
            pltpu.VMEM((2 * rows, width), BF16),
            pltpu.VMEM((keys, width), BF16),
            pltpu.VMEM((keys, 2 * rows), BF16),
            pltpu.VMEM((1, rows), I32),
            pltpu.VMEM((1, rows), I32),
            pltpu.VMEM((8, 2 * rows), F32),
            pltpu.VMEM((8, 2 * rows), F32),
            pltpu.SemaphoreType.DMA((3,)),
            pltpu.SemaphoreType.DMA((n,)),
            pltpu.SemaphoreType.DMA((parts,)),
            pltpu.SemaphoreType.DMA((parts,)),
        ],
        compiler_params=params(SCOPE),
        cost_estimate=cost(2 * keys * 2 * rows * width, 4e6, keys * 2 * rows),
        name="logits",
    )(*args)


def log_total(here, there):
    m, l = merge(here[0:1, :], here[1:2, :], there[0:1, :], there[1:2, :])
    return m + jnp.log(l)


def weights_kernel(chunks, *refs):
    n = len(chunks)
    total = sum(len(chunk) for chunk in chunks)
    at_ref, refs = refs[0], refs[1:]
    far, refs = refs[: 4 + n], refs[4 + n :]
    e_refs, (qa_ref, qb_ref), refs = refs[:n], refs[n : n + 2], refs[n + 2 :]
    w_refs, g_refs, stamp_ref, refs = refs[:n], refs[n : 2 * n], refs[2 * n], refs[2 * n + 1 :]
    q, w, g = refs[:3]
    near, (s_sem, e_sem, q_sem, w_sem, g_sem) = refs[3 : 7 + n], refs[7 + n :]
    rows, width = qa_ref.shape
    p_rows = g.shape[0] // total
    tiles = query_tiles(rows)
    spans, start = [], 0
    for chunk in chunks:
        spans.append((start, len(chunk) * p_rows))
        start += len(chunk) * p_rows
    small = fetch(zip(far, near), s_sem)
    pos_refs, here_ref, there_ref, stat_refs = near[:2], near[2], near[3], near[4:]
    loads = []
    for i, (side, here, at, _) in enumerate(tiles):
        group = [
            pltpu.make_async_copy(e_refs[c].at[:, at], w.at[pl.ds(first, size), at], e_sem.at[c, i])
            for c, (first, size) in enumerate(spans)
        ]
        group.append(pltpu.make_async_copy((qa_ref, qb_ref)[side].at[here, :], q.at[at, :], q_sem.at[i]))
        loads.append(group)
    for copy in loads[0] + loads[1]:
        copy.start()
    stamp_ref[...] = jnp.zeros_like(stamp_ref)
    for copy in small:
        copy.wait()
    out = []
    for i, (side, here, at, over) in enumerate(tiles):
        lse = log_total(here_ref[:, at], there_ref[:, over])
        hit = jnp.exp(here_ref[2:3, at] - lse) - 1.0
        pos = pos_refs[side][0:1, here]
        for copy in loads[i]:
            copy.wait()
        if i + 2 < len(tiles):
            for copy in loads[i + 2]:
                copy.start()
        for c, chunk in enumerate(chunks):
            first, size = spans[c]
            scale = jnp.exp(stat_refs[c][0:1, at] - lse)
            for b, offset in enumerate(chunk):
                down = slice(first + b * p_rows, first + (b + 1) * p_rows)
                p = w[down, at].astype(F32) * scale
                mark = pos - key_ids(at_ref, offset, p_rows)
                w[down, at] = jnp.where(iota(p.shape, 0) == mark, hit, p).astype(BF16)
            span = slice(first, first + size)
            out.append(pltpu.make_async_copy(w.at[span, at], w_refs[c].at[:, at], w_sem.at[c, i]))
            out[-1].start()
            for part in range(width // WIDE):
                cols = slice(part * WIDE, (part + 1) * WIDE)
                term = dot(w[span, at], q[at, cols], ((1,), (0,)))
                g[span, cols] = term if i == 0 else g[span, cols] + term
            if i == len(tiles) - 1:
                out.append(pltpu.make_async_copy(g.at[span, :], g_refs[c], g_sem.at[c]))
                out[-1].start()
    for copy in out:
        copy.wait()


def weights(chunks, at, pa, pb, here, there, stats, es, qa, qb):
    rows, width = qa.shape
    n = len(chunks)
    keys = sum(e.shape[0] for e in es)
    parts = 2 * rows // TILE
    stat = pltpu.VMEM((8, 2 * rows), F32)
    out = pl.pallas_call(
        functools.partial(weights_kernel, chunks),
        out_shape=tuple(jax.ShapeDtypeStruct(e.shape, BF16) for e in es)
        + tuple(jax.ShapeDtypeStruct((e.shape[0], width), F32) for e in es)
        + (jax.ShapeDtypeStruct(STAMP, F32),),
        in_specs=[SMEM] + [HBM] * (6 + 2 * n),
        out_specs=(HBM,) * (2 * n) + (VMEM,),
        scratch_shapes=[
            pltpu.VMEM((2 * rows, width), BF16),
            pltpu.VMEM((keys, 2 * rows), BF16),
            pltpu.VMEM((keys, width), F32),
            pltpu.VMEM((1, rows), I32),
            pltpu.VMEM((1, rows), I32),
        ]
        + [stat] * (2 + n)
        + [
            pltpu.SemaphoreType.DMA((4 + n,)),
            pltpu.SemaphoreType.DMA((n, parts)),
            pltpu.SemaphoreType.DMA((parts,)),
            pltpu.SemaphoreType.DMA((n, parts)),
            pltpu.SemaphoreType.DMA((n,)),
        ],
        compiler_params=params(SCOPE),
        cost_estimate=cost(2 * keys * 2 * rows * width, 4e6, keys * 2 * rows),
        name="weights",
    )(at, pa, pb, here, there, *stats, *es, qa, qb)
    return out[:n], out[n : 2 * n], out[2 * n]


def mined_weights_kernel(cap, here_ref, there_ref, stat_ref, e_ref, q_ref, pick_ref, _, w_ref, back_ref, loss_ref, stamp_ref):
    rows, width = q_ref.shape
    here, there = here_ref[:, :rows], there_ref[:, rows:]
    lse = log_total(here, there)
    loss_ref[...] = lse - here[2:3, :] - there[2:3, :]
    w = (e_ref[...].astype(F32) * jnp.exp(stat_ref[0:1, :rows] - lse)).astype(BF16)
    w_ref[...] = w
    g = dot(w, q_ref[...], ((1,), (0,))).astype(BF16)
    pick = pick_ref[...]
    first = dot(pick, g[:, : width // 2], ((1,), (0,)))
    second = dot(pick, g[:, width // 2 :], ((1,), (0,)))
    low = (iota(first.shape, 0) % (2 * cap)) < cap
    back_ref[...] = jnp.where(low, first, second).astype(BF16)
    stamp_ref[...] = jnp.zeros_like(stamp_ref)


def mined_weights(here, there, stat, e, q, pick, cap, after):
    count, rows = e.shape
    width = q.shape[1]
    slots = pick.shape[0]
    outs = (
        jax.ShapeDtypeStruct((count, rows), BF16),
        jax.ShapeDtypeStruct((slots, width // 2), BF16),
        jax.ShapeDtypeStruct((1, rows), F32),
        jax.ShapeDtypeStruct(STAMP, F32),
    )
    body = functools.partial(mined_weights_kernel, cap)
    return staged(body, "mined_weights", (here, there, stat, e, q, pick, after), outs, 1.4e9)


def query_kernel(counts, side, tile, adds, *refs):
    chunks = len(counts)
    w_refs, refs = refs[:chunks], refs[chunks:]
    k_refs, refs = refs[: sum(counts)], refs[sum(counts) :]
    x_refs, refs = refs[:adds], refs[adds:]
    out_refs, (stamp_ref, w, k, x, acc, w_sem, k_sem, x_sem, o_sem) = refs[:-9], refs[-9:]
    rows = acc.shape[0]
    parts = rows // tile
    stamp_ref[...] = jnp.zeros_like(stamp_ref)
    copies, spans, start, block = [], [], 0, 0
    for c, count in enumerate(counts):
        depth = w_refs[c].shape[0]
        left = side * rows if w_refs[c].shape[1] > rows else 0
        pending = [pltpu.make_async_copy(w_refs[c].at[:, pl.ds(left, rows)], w.at[pl.ds(start, depth), :], w_sem.at[c])]
        for i in range(count):
            ref = k_refs[block + i]
            size = ref.shape[0]
            to = k.at[pl.ds(start + i * size, size), :]
            pending.append(pltpu.make_async_copy(ref, to, k_sem.at[block + i]))
        for copy in pending:
            copy.start()
        copies.append(pending)
        spans.append(slice(start, start + depth))
        start, block = start + depth, block + count
    spans_x = [pl.ds(i * tile, tile) for i in range(parts)] if adds else []
    more = fetch([(x_refs[0].at[at, :], x.at[at, :]) for at in spans_x], x_sem)
    out = []
    for c, span in enumerate(spans):
        for copy in copies[c]:
            copy.wait()
        for part in range(parts):
            at = slice(part * tile, (part + 1) * tile)
            term = dot(w[span, at], k[span, :], ((0,), (0,)))
            if c > 0:
                term = term + acc[at, :]
            if c == chunks - 1:
                if adds:
                    more[part].wait()
                    term = term + x[at, :]
            acc[at, :] = term
            if c == chunks - 1:
                to = out_refs[part] if len(out_refs) > 1 else out_refs[0].at[at, :]
                out.append(pltpu.make_async_copy(acc.at[at, :], to, o_sem.at[part]))
                out[-1].start()
    for copy in out:
        copy.wait()


def query_grad(ws, blocks, side, rows, extras, split):
    width = blocks[0][0].shape[1]
    tile = 256
    parts = rows // tile
    flat = [b for group in blocks for b in group]
    depth = sum(w.shape[0] for w in ws)
    shapes = [jax.ShapeDtypeStruct((tile, width), F32)] * parts if split else [jax.ShapeDtypeStruct((rows, width), F32)]
    out = pl.pallas_call(
        functools.partial(query_kernel, tuple(len(group) for group in blocks), side, tile, len(extras)),
        out_shape=tuple(shapes) + (jax.ShapeDtypeStruct(STAMP, F32),),
        in_specs=[HBM] * (len(ws) + len(flat) + len(extras)),
        out_specs=(HBM,) * len(shapes) + (VMEM,),
        scratch_shapes=[
            pltpu.VMEM((depth, rows), BF16),
            pltpu.VMEM((depth, width), BF16),
            pltpu.VMEM((rows if extras else 8, width), F32),
            pltpu.VMEM((rows, width), F32),
            pltpu.SemaphoreType.DMA((len(ws),)),
            pltpu.SemaphoreType.DMA((len(flat),)),
            pltpu.SemaphoreType.DMA((parts,)),
            pltpu.SemaphoreType.DMA((parts,)),
        ],
        compiler_params=params(SCOPE),
        cost_estimate=cost(2 * rows * width * depth, 6e6),
        name="query_grad",
    )(*ws, *flat, *extras)
    return out[:-1], out[-1]


def owned_kernel(cap, hot_ref, back_ref, out_ref):
    hot = hot_ref[...]
    half = back_ref.shape[1]
    for h in range(2):
        out_ref[:, h * half : (h + 1) * half] = dot(half_rows(hot, cap, h), back_ref[...], ((0,), (0,)))


def owned_sum(hot, back, cap):
    outs = (jax.ShapeDtypeStruct((hot.shape[1], 2 * back.shape[1]), F32),)
    return staged(functools.partial(owned_kernel, cap), "owned_sum", (hot, back), outs, 4e8)[0]


def tie(values, *others):
    return lax.optimization_barrier((values, others))[0]


def local(queries, passages, mined_owner, mined_row, positives):
    groups = lax.axis_size("group")
    devs = lax.axis_size("dev")
    total = groups * devs
    dev = lax.axis_index("dev")
    me = lax.axis_index("group") * devs + dev
    at = jnp.stack([dev // (2 * SIDE), (dev // 2) % SIDE, dev % 2]).astype(I32)
    rows, width = queries.shape
    cap = max(2, 2 * (mined_owner.shape[0] // total) // total)

    other = swap(queries)
    pa = positives.reshape(1, rows)
    pb = swap(pa)

    def exchange(value):
        value = value.reshape(total, 2 * cap, width // 2)
        value = lax.all_to_all(value, ("group", "dev"), split_axis=0, concat_axis=0, tiled=True)
        return value.reshape(total * 2 * cap, width // 2)

    held = {wrap(OWN): passages}

    def source(to, step):
        return wrap((to[0] - step[0], to[1] - step[1]))

    def spread(stage, *others):
        names = [source(to, step) for to, step in stage]
        values = tie([held[n] for n in names], *others) if others else [held[n] for n in names]
        for (to, step), value in zip(stage, values):
            held[wrap(to)] = shift(value, step)

    def round_of(number):
        return [held[wrap(to)] for to, _ in ROUNDS[number]]

    spread(ROUNDS[0])
    owners = mined_owner[:, 0].reshape(total, -1)
    names = mined_row.reshape(total, -1)
    outgoing, hot, pick = serve(me.astype(I32).reshape(1, 1), owners, names, passages, cap)
    arrived = exchange(outgoing)
    blocks = lambda chunk: [held[wrap(o)] for o in chunk]
    spread(ROUNDS[1], owners, names, round_of(0))
    spread(ROUNDS[2], round_of(1), round_of(0))
    near = CHUNKS[0] + CHUNKS[1]
    e1, stat1 = logits(near, at, pa, pb, queries, other, blocks(near), None)
    spread(ROUNDS[3], stat1, round_of(2))
    mined, e_mined, stat_mined = mined_logits(arrived, pick, queries, stat1, cap)
    far = CHUNKS[2] + CHUNKS[3]
    e2, stat = logits(far, at, pa, pb, queries, other, blocks(far), stat_mined)
    there = swap(stat)

    grads = {}

    def collect(number, g, *stamps):
        chunk, stage = CHUNKS[number], ROUNDS[number]
        n = passages.shape[0]
        for b, o in enumerate(chunk):
            grads.setdefault(wrap(o), []).insert(0, g[b * n : (b + 1) * n])
        zeros = [stamp.reshape(()) for stamp in stamps]
        for to, step in stage:
            send = functools.reduce(jnp.add, [v.astype(F32) for v in grads[wrap(to)]] + zeros).astype(LINK)
            grads.setdefault(source(to, step), []).append(shift(send, (-step[0], -step[1])))

    groups_of = (near, far)
    ws, (g1, g2), w_done = weights(groups_of, at, pa, pb, stat, there, (stat1, stat), (e1, e2), queries, other)
    split = len(CHUNKS[0]) * passages.shape[0]
    ks = [blocks(group) for group in groups_of]
    collect(3, g2[split:])
    theirs, their_done = query_grad(ws, ks, 1, rows, (), False)
    theirs = swap(theirs[0])
    collect(2, g2[:split], their_done)
    w_mined, back, losses, mined_done = mined_weights(stat, there, stat_mined, e_mined, queries, pick, cap, their_done)
    returned = exchange(back)
    collect(1, g1[split:], mined_done)
    (mine,), own_done = query_grad([*ws, w_mined], ks + [[mined]], 0, rows, (theirs,), False)
    collect(0, g1[:split], own_done)
    owned = owned_sum(hot, returned, cap)
    passage = functools.reduce(jnp.add, [v.astype(F32) for v in grads[wrap(OWN)]] + [owned])
    return losses.reshape(rows), mine, passage


def solution(mesh):
    placed = (P(("group", "dev"), None), P(("group", "dev"), None), P(), P(), P(("group", "dev")))
    return jax.shard_map(
        local,
        mesh=mesh,
        in_specs=placed,
        out_specs=(P(("group", "dev")), P(("group", "dev"), None), P(("group", "dev"), None)),
        check_vma=False,
    )
```

```python
import functools

import jax
import jax.numpy as jnp
from jax import lax
from jax.experimental import pallas as pl
from jax.experimental.pallas import tpu as pltpu
from jax.sharding import PartitionSpec as P

F32 = jnp.float32
BF16 = jnp.bfloat16
I32 = jnp.int32
LINK = jnp.float16
SIDE = 4
TILE = 512
WIDE = 512
SCOPE = 60
SMALL = 24
MIB = 1 << 20
WEIGHT = 2.5

ROUNDS = (
    (((1, 0), (1, 0)), ((-1, 0), (-1, 0)), ((0, 1), (0, 1)), ((0, -1), (0, -1))),
    (((1, 1), (0, 1)), ((1, -1), (1, 0)), ((-1, -1), (-1, 0))),
    (((2, 1), (1, 0)), ((2, 0), (-1, 0)), ((-1, 1), (0, 1)), ((0, 2), (0, -1))),
    (((2, 2), (0, 1)), ((2, -1), (-1, 0)), ((1, 2), (1, 0)), ((-1, 2), (0, -1))),
)
OWN = (0, 0)
CHUNKS = (
    tuple(to for to, _ in ROUNDS[0]),
    (OWN,) + tuple(to for to, _ in ROUNDS[1]),
    tuple(to for to, _ in ROUNDS[2]),
    tuple(to for to, _ in ROUNDS[3]),
)


def wrap(offset):
    return (offset[0] % SIDE, offset[1] % SIDE)


def shift(value, step):
    pairs = []
    for x in range(SIDE):
        for y in range(SIDE):
            for core in range(2):
                there = ((x + step[0]) % SIDE) * SIDE + (y + step[1]) % SIDE
                pairs.append(((x * SIDE + y) * 2 + core, there * 2 + core))
    return lax.ppermute(value, "dev", pairs)


def swap(value):
    return lax.ppermute(value, "dev", [(i, i ^ 1) for i in range(2 * SIDE * SIDE)])


def dot(a, b, dims):
    return lax.dot_general(a, b, (dims, ((), ())), preferred_element_type=F32)


def iota(shape, axis):
    return lax.broadcasted_iota(I32, shape, axis)


def params(mib):
    return pltpu.CompilerParams(vmem_limit_bytes=mib * MIB)


def cost(flops, moved, exps=0):
    return pl.CostEstimate(flops=int(flops * WEIGHT), bytes_accessed=int(moved * WEIGHT), transcendentals=int(exps))


VMEM = pl.BlockSpec(memory_space=pltpu.VMEM)
SMEM = pl.BlockSpec(memory_space=pltpu.SMEM)
HBM = pl.BlockSpec(memory_space=pltpu.HBM)
STAMP = (1, 1)


def staged(body, name, operands, outs, flops):
    n, count = len(operands), len(outs)

    def kernel(*refs):
        sources, targets = refs[:n], refs[n : n + count]
        inner, results = refs[n + count : 2 * n + count], refs[2 * n + count : 2 * (n + count)]
        in_sem, out_sem = refs[2 * (n + count) :]
        for copy in fetch(zip(sources, inner), in_sem):
            copy.wait()
        body(*inner, *results)
        for copy in fetch(zip(results, targets), out_sem):
            copy.wait()

    return pl.pallas_call(
        kernel,
        out_shape=tuple(outs),
        in_specs=[HBM] * n,
        out_specs=(HBM,) * count,
        scratch_shapes=[pltpu.VMEM(v.shape, v.dtype) for v in (*operands, *outs)]
        + [pltpu.SemaphoreType.DMA((n,)), pltpu.SemaphoreType.DMA((count,))],
        compiler_params=params(SMALL),
        cost_estimate=cost(flops, 4e6),
        name=name,
    )(*operands)


def ahead(pairs, sems):
    return [pltpu.make_async_copy(source, to, sems.at[i]) for i, (source, to) in enumerate(pairs)]


def fetch(pairs, sems):
    copies = ahead(pairs, sems)
    for copy in copies:
        copy.start()
    return copies


def serve_kernel(cap, me_ref, owners_ref, rows_ref, pass_ref, out_ref, hot_ref, pick_ref):
    me = me_ref[...]
    total, count = owners_ref.shape
    p_rows, width = pass_ref.shape
    deep = 2 * cap
    slots = total * deep
    earlier = (iota((count, count), 0) < iota((count, count), 1)).astype(BF16)
    asked = (owners_ref[...] == me).astype(F32)
    order = dot(asked.astype(BF16), earlier, ((1,), (0,)))
    rows = rows_ref[...].astype(F32)
    lane = iota((total, 128), 1)
    table = jnp.zeros((total, 128), F32)
    for place in range(cap):
        chosen = jnp.where(order == float(place), asked, 0.0)
        table += jnp.where(lane % cap == place, jnp.sum(chosen * rows, axis=1, keepdims=True), 0.0)
    spread = ((iota((slots, total), 0) // deep) == iota((slots, total), 1)).astype(BF16)
    wide = dot(spread, table.astype(BF16), ((1,), (0,)))
    mine = (iota((slots, 128), 0) % deep) == iota((slots, 128), 1)
    wanted = jnp.sum(jnp.where(mine, wide, 0.0), axis=1, keepdims=True)
    hot = (iota((slots, p_rows), 1).astype(F32) == wanted).astype(BF16)
    hot_ref[...] = hot
    first = dot(hot, pass_ref[:, : width // 2], ((1,), (0,)))
    second = dot(hot, pass_ref[:, width // 2 :], ((1,), (0,)))
    low = (iota(first.shape, 0) % deep) < cap
    out_ref[...] = jnp.where(low, first, second).astype(BF16)
    mine_row = iota((total, count), 0) == me
    own = jnp.sum(jnp.where(mine_row, owners_ref[...], 0), axis=0, keepdims=True)
    hits = (iota((total, count), 0) == own).astype(F32)
    before = dot(hits.astype(BF16), earlier, ((1,), (0,)))
    place = jnp.sum(hits * before, axis=0, keepdims=True).astype(I32)
    row = iota((slots, count), 0)
    fetch = own * deep + place
    pick_ref[...] = ((row == fetch) | (row == fetch + cap)).astype(BF16)


def serve(me, owners, rows, passages, cap):
    total, count = owners.shape
    p_rows, width = passages.shape
    slots = total * 2 * cap
    outs = (
        jax.ShapeDtypeStruct((slots, width // 2), BF16),
        jax.ShapeDtypeStruct((slots, p_rows), BF16),
        jax.ShapeDtypeStruct((slots, count), BF16),
    )
    body = functools.partial(serve_kernel, cap)
    return staged(body, "serve_mined", (me, owners, rows, passages), outs, 8e8)


def half_rows(pick, cap, half):
    keep = ((iota(pick.shape, 0) % (2 * cap)) < cap) == (half == 0)
    return jnp.where(keep, pick, jnp.zeros_like(pick))


def merge(m_a, l_a, m_b, l_b):
    m = jnp.maximum(m_a, m_b)
    return m, l_a * jnp.exp(m_a - m) + l_b * jnp.exp(m_b - m)


def mined_logits_kernel(cap, got_ref, pick_ref, q_ref, old_ref, keys_ref, e_ref, stat_ref):
    rows, width = q_ref.shape
    pick = pick_ref[...]
    for h in range(2):
        part = dot(half_rows(pick, cap, h), got_ref[...], ((0,), (0,)))
        keys_ref[:, h * (width // 2) : (h + 1) * (width // 2)] = part.astype(BF16)
    stat_ref[...] = old_ref[...]
    for part in range(rows // TILE):
        at = slice(part * TILE, (part + 1) * TILE)
        s = dot(keys_ref[...], q_ref[at, :], ((1,), (1,)))
        m_old = old_ref[0:1, at]
        m = jnp.maximum(jnp.max(s, axis=0, keepdims=True), m_old)
        e = jnp.exp(s - m)
        e_ref[:, at] = e.astype(BF16)
        stat_ref[0:1, at] = m
        stat_ref[1:2, at] = jnp.sum(e, axis=0, keepdims=True) + old_ref[1:2, at] * jnp.exp(m_old - m)


def mined_logits(got, pick, q, old, cap):
    count = pick.shape[1]
    rows, width = q.shape
    outs = (
        jax.ShapeDtypeStruct((count, width), BF16),
        jax.ShapeDtypeStruct((count, rows), BF16),
        jax.ShapeDtypeStruct((8, 2 * rows), F32),
    )
    return staged(functools.partial(mined_logits_kernel, cap), "mined_logits", (got, pick, q, old), outs, 1.6e9)


def key_ids(at_ref, offset, p_rows):
    x = (at_ref[0] + (SIDE - offset[0])) % SIDE
    y = (at_ref[1] + (SIDE - offset[1])) % SIDE
    return ((x * SIDE + y) * 2 + at_ref[2]) * p_rows


def query_tiles(rows):
    tiles = []
    for side in range(2):
        for part in range(rows // TILE):
            here = slice(part * TILE, (part + 1) * TILE)
            at = slice(side * rows + part * TILE, side * rows + (part + 1) * TILE)
            far = slice((1 - side) * rows + part * TILE, (1 - side) * rows + (part + 1) * TILE)
            tiles.append((side, here, at, far))
    return tiles


def logits_kernel(chunk, first, *refs):
    at_ref, pa_ref, pb_ref = refs[:3]
    blocks = len(chunk)
    rest = list(refs[3:])
    far_refs = [pa_ref, pb_ref] + ([] if first else [rest.pop(0)])
    qa_ref, qb_ref = rest[:2]
    k_refs = rest[2 : 2 + blocks]
    e_ref, far_stat_ref, q, k, e, pos_a, pos_b, old, stat, s_sem, k_sem, q_sem, e_sem = rest[2 + blocks :]
    small = fetch(zip(far_refs, (pos_a, pos_b, old)), s_sem)
    pa_ref, pb_ref, old_ref, stat_ref = pos_a, pos_b, old, stat
    p_rows = k_refs[0].shape[0]
    rows = qa_ref.shape[0]
    tiles = query_tiles(rows)
    k_copies = fetch([(k_refs[b], k.at[pl.ds(b * p_rows, p_rows), :]) for b in range(blocks)], k_sem)
    q_copies = ahead([((qa_ref, qb_ref)[side].at[here, :], q.at[at, :]) for side, here, at, _ in tiles], q_sem)
    q_copies[0].start()
    q_copies[1].start()
    base = [key_ids(at_ref, o, p_rows) for o in chunk]
    stat_ref[...] = jnp.zeros_like(stat_ref)
    for copy in small + k_copies:
        copy.wait()
    out = []
    for i, (side, here, at, _) in enumerate(tiles):
        q_copies[i].wait()
        if i + 2 < len(tiles):
            q_copies[i + 2].start()
        s = dot(k[...], q[at, :], ((1,), (1,)))
        m = jnp.max(s, axis=0, keepdims=True)
        if not first:
            m = jnp.maximum(m, old_ref[0:1, at])
        p = jnp.exp(s - m)
        e[:, at] = p.astype(BF16)
        out.append(pltpu.make_async_copy(e.at[:, at], e_ref.at[:, at], e_sem.at[i]))
        out[-1].start()
        l = jnp.sum(p, axis=0, keepdims=True)
        pos = (pa_ref, pb_ref)[side][0:1, here]
        t = jnp.zeros_like(m)
        for b in range(blocks):
            piece = s[b * p_rows : (b + 1) * p_rows, :]
            t += jnp.sum(jnp.where(iota(piece.shape, 0) == pos - base[b], piece, 0.0), axis=0, keepdims=True)
        if not first:
            l += old_ref[1:2, at] * jnp.exp(old_ref[0:1, at] - m)
            t += old_ref[2:3, at]
        stat_ref[0:1, at] = m
        stat_ref[1:2, at] = l
        stat_ref[2:3, at] = t
    out += fetch([(stat, far_stat_ref)], s_sem)
    for copy in out:
        copy.wait()


def logits(chunk, at, pa, pb, qa, qb, blocks, old):
    rows, width = qa.shape
    n = len(blocks)
    keys = n * blocks[0].shape[0]
    parts = 2 * rows // TILE
    args = [at, pa, pb] + ([] if old is None else [old]) + [qa, qb, *blocks]
    return pl.pallas_call(
        functools.partial(logits_kernel, chunk, old is None),
        out_shape=(jax.ShapeDtypeStruct((keys, 2 * rows), BF16), jax.ShapeDtypeStruct((8, 2 * rows), F32)),
        in_specs=[SMEM] + [HBM] * (len(args) - 1),
        out_specs=(HBM, HBM),
        scratch_shapes=[
            pltpu.VMEM((2 * rows, width), BF16),
            pltpu.VMEM((keys, width), BF16),
            pltpu.VMEM((keys, 2 * rows), BF16),
            pltpu.VMEM((1, rows), I32),
            pltpu.VMEM((1, rows), I32),
            pltpu.VMEM((8, 2 * rows), F32),
            pltpu.VMEM((8, 2 * rows), F32),
            pltpu.SemaphoreType.DMA((3,)),
            pltpu.SemaphoreType.DMA((n,)),
            pltpu.SemaphoreType.DMA((parts,)),
            pltpu.SemaphoreType.DMA((parts,)),
        ],
        compiler_params=params(SCOPE),
        cost_estimate=cost(2 * keys * 2 * rows * width, 4e6, keys * 2 * rows),
        name="logits",
    )(*args)


def log_total(here, there):
    m, l = merge(here[0:1, :], here[1:2, :], there[0:1, :], there[1:2, :])
    return m + jnp.log(l)


def weights_kernel(chunks, *refs):
    n = len(chunks)
    total = sum(len(chunk) for chunk in chunks)
    at_ref, refs = refs[0], refs[1:]
    far, refs = refs[: 4 + n], refs[4 + n :]
    e_refs, (qa_ref, qb_ref), refs = refs[:n], refs[n : n + 2], refs[n + 2 :]
    k_refs, refs = refs[:total], refs[total:]
    g_refs, sides, stamp_ref, refs = refs[:n], refs[n : n + 2], refs[n + 2], refs[n + 3 :]
    q, w, g, k, d = refs[:5]
    near, (s_sem, e_sem, q_sem, k_sem, d_sem, g_sem) = refs[5 : 9 + n], refs[9 + n :]
    rows, width = qa_ref.shape
    p_rows = g.shape[0] // total
    tiles = query_tiles(rows)
    spans, start = [], 0
    for chunk in chunks:
        spans.append((start, len(chunk) * p_rows))
        start += len(chunk) * p_rows
    small = fetch(zip(far, near), s_sem)
    pos_refs, here_ref, there_ref, stat_refs = near[:2], near[2], near[3], near[4:]
    loads = []
    for i, (side, here, at, _) in enumerate(tiles):
        group = [
            pltpu.make_async_copy(e_refs[c].at[:, at], w.at[pl.ds(first, size), at], e_sem.at[c, i])
            for c, (first, size) in enumerate(spans)
        ]
        group.append(pltpu.make_async_copy((qa_ref, qb_ref)[side].at[here, :], q.at[at, :], q_sem.at[i]))
        loads.append(group)
    for copy in loads[0]:
        copy.start()
    k_copies = fetch([(k_refs[b], k.at[pl.ds(b * p_rows, p_rows), :]) for b in range(total)], k_sem)
    for copy in loads[1]:
        copy.start()
    stamp_ref[...] = jnp.zeros_like(stamp_ref)
    for copy in small:
        copy.wait()
    out, turns = [], []
    for i, (side, here, at, over) in enumerate(tiles):
        lse = log_total(here_ref[:, at], there_ref[:, over])
        hit = jnp.exp(here_ref[2:3, at] - lse) - 1.0
        pos = pos_refs[side][0:1, here]
        for copy in loads[i]:
            copy.wait()
        if i + 2 < len(tiles):
            for copy in loads[i + 2]:
                copy.start()
        for c, chunk in enumerate(chunks):
            first, size = spans[c]
            scale = jnp.exp(stat_refs[c][0:1, at] - lse)
            for b, offset in enumerate(chunk):
                down = slice(first + b * p_rows, first + (b + 1) * p_rows)
                p = w[down, at].astype(F32) * scale
                mark = pos - key_ids(at_ref, offset, p_rows)
                w[down, at] = jnp.where(iota(p.shape, 0) == mark, hit, p).astype(BF16)
            span = slice(first, first + size)
            for part in range(width // WIDE):
                cols = slice(part * WIDE, (part + 1) * WIDE)
                term = dot(w[span, at], q[at, cols], ((1,), (0,)))
                g[span, cols] = term if i == 0 else g[span, cols] + term
            if i == len(tiles) - 1:
                out.append(pltpu.make_async_copy(g.at[span, :], g_refs[c], g_sem.at[c]))
                out[-1].start()
        if i == 0:
            for copy in k_copies:
                copy.wait()
        if i >= 2:
            turns[i - 2].wait()
        d[i % 2] = dot(w[:, at], k[...], ((0,), (0,)))
        turns.append(pltpu.make_async_copy(d.at[i % 2], sides[side].at[here, :], d_sem.at[i % 2]))
        turns[-1].start()
    for copy in out + turns[-2:]:
        copy.wait()


def weights(chunks, at, pa, pb, here, there, stats, es, qa, qb, blocks):
    rows, width = qa.shape
    n = len(chunks)
    keys = sum(e.shape[0] for e in es)
    parts = 2 * rows // TILE
    stat = pltpu.VMEM((8, 2 * rows), F32)
    out = pl.pallas_call(
        functools.partial(weights_kernel, chunks),
        out_shape=tuple(jax.ShapeDtypeStruct((e.shape[0], width), F32) for e in es)
        + (jax.ShapeDtypeStruct((rows, width), F32),) * 2
        + (jax.ShapeDtypeStruct(STAMP, F32),),
        in_specs=[SMEM] + [HBM] * (6 + 2 * n + len(blocks)),
        out_specs=(HBM,) * (n + 2) + (VMEM,),
        scratch_shapes=[
            pltpu.VMEM((2 * rows, width), BF16),
            pltpu.VMEM((keys, 2 * rows), BF16),
            pltpu.VMEM((keys, width), F32),
            pltpu.VMEM((keys, width), BF16),
            pltpu.VMEM((2, TILE, width), F32),
            pltpu.VMEM((1, rows), I32),
            pltpu.VMEM((1, rows), I32),
        ]
        + [stat] * (2 + n)
        + [
            pltpu.SemaphoreType.DMA((4 + n,)),
            pltpu.SemaphoreType.DMA((n, parts)),
            pltpu.SemaphoreType.DMA((parts,)),
            pltpu.SemaphoreType.DMA((len(blocks),)),
            pltpu.SemaphoreType.DMA((2,)),
            pltpu.SemaphoreType.DMA((n,)),
        ],
        compiler_params=params(SCOPE),
        cost_estimate=cost(4 * keys * 2 * rows * width, 4e6, keys * 2 * rows),
        name="weights",
    )(at, pa, pb, here, there, *stats, *es, qa, qb, *blocks)
    return out[:n], out[n], out[n + 1], out[n + 2]


def mined_weights_kernel(cap, here_ref, there_ref, stat_ref, e_ref, q_ref, pick_ref, _, w_ref, back_ref, loss_ref, stamp_ref):
    rows, width = q_ref.shape
    here, there = here_ref[:, :rows], there_ref[:, rows:]
    lse = log_total(here, there)
    loss_ref[...] = lse - here[2:3, :] - there[2:3, :]
    w = (e_ref[...].astype(F32) * jnp.exp(stat_ref[0:1, :rows] - lse)).astype(BF16)
    w_ref[...] = w
    g = dot(w, q_ref[...], ((1,), (0,))).astype(BF16)
    pick = pick_ref[...]
    first = dot(pick, g[:, : width // 2], ((1,), (0,)))
    second = dot(pick, g[:, width // 2 :], ((1,), (0,)))
    low = (iota(first.shape, 0) % (2 * cap)) < cap
    back_ref[...] = jnp.where(low, first, second).astype(BF16)
    stamp_ref[...] = jnp.zeros_like(stamp_ref)


def mined_weights(here, there, stat, e, q, pick, cap, after):
    count, rows = e.shape
    width = q.shape[1]
    slots = pick.shape[0]
    outs = (
        jax.ShapeDtypeStruct((count, rows), BF16),
        jax.ShapeDtypeStruct((slots, width // 2), BF16),
        jax.ShapeDtypeStruct((1, rows), F32),
        jax.ShapeDtypeStruct(STAMP, F32),
    )
    body = functools.partial(mined_weights_kernel, cap)
    return staged(body, "mined_weights", (here, there, stat, e, q, pick, after), outs, 1.4e9)


def finish_kernel(tile, own_ref, their_ref, w_ref, k_ref, out_ref, stamp_ref, own, their, w, k, a_sem, b_sem, w_sem, o_sem):
    rows = own.shape[0]
    spans = [pl.ds(i * tile, tile) for i in range(rows // tile)]
    small = fetch([(w_ref, w), (k_ref, k)], w_sem)
    first = fetch([(own_ref.at[at, :], own.at[at, :]) for at in spans], a_sem)
    second = fetch([(their_ref.at[at, :], their.at[at, :]) for at in spans], b_sem)
    stamp_ref[...] = jnp.zeros_like(stamp_ref)
    for copy in small:
        copy.wait()
    out = []
    for i in range(rows // tile):
        at = slice(i * tile, (i + 1) * tile)
        term = dot(w[:, at], k[...], ((0,), (0,)))
        first[i].wait()
        second[i].wait()
        own[at, :] = own[at, :] + their[at, :] + term
        out.append(pltpu.make_async_copy(own.at[spans[i], :], out_ref.at[spans[i], :], o_sem.at[i]))
        out[-1].start()
    for copy in out:
        copy.wait()


def finish(own, theirs, w, k):
    rows, width = own.shape
    tile = 256
    parts = rows // tile
    return pl.pallas_call(
        functools.partial(finish_kernel, tile),
        out_shape=(jax.ShapeDtypeStruct((rows, width), F32), jax.ShapeDtypeStruct(STAMP, F32)),
        in_specs=[HBM] * 4,
        out_specs=(HBM, VMEM),
        scratch_shapes=[
            pltpu.VMEM((rows, width), F32),
            pltpu.VMEM((rows, width), F32),
            pltpu.VMEM(w.shape, BF16),
            pltpu.VMEM(k.shape, BF16),
            pltpu.SemaphoreType.DMA((parts,)),
            pltpu.SemaphoreType.DMA((parts,)),
            pltpu.SemaphoreType.DMA((2,)),
            pltpu.SemaphoreType.DMA((parts,)),
        ],
        compiler_params=params(SCOPE),
        cost_estimate=cost(2 * rows * width * k.shape[0], 1.3e7),
        name="finish",
    )(own, theirs, w, k)


def owned_kernel(cap, hot_ref, back_ref, out_ref):
    hot = hot_ref[...]
    half = back_ref.shape[1]
    for h in range(2):
        out_ref[:, h * half : (h + 1) * half] = dot(half_rows(hot, cap, h), back_ref[...], ((0,), (0,)))


def owned_sum(hot, back, cap):
    outs = (jax.ShapeDtypeStruct((hot.shape[1], 2 * back.shape[1]), F32),)
    return staged(functools.partial(owned_kernel, cap), "owned_sum", (hot, back), outs, 4e8)[0]


def tie(values, *others):
    return lax.optimization_barrier((values, others))[0]


def local(queries, passages, mined_owner, mined_row, positives):
    groups = lax.axis_size("group")
    devs = lax.axis_size("dev")
    total = groups * devs
    dev = lax.axis_index("dev")
    me = lax.axis_index("group") * devs + dev
    at = jnp.stack([dev // (2 * SIDE), (dev // 2) % SIDE, dev % 2]).astype(I32)
    rows, width = queries.shape
    cap = max(2, 2 * (mined_owner.shape[0] // total) // total)

    other = swap(queries)
    pa = positives.reshape(1, rows)
    pb = swap(pa)

    def exchange(value):
        value = value.reshape(total, 2 * cap, width // 2)
        value = lax.all_to_all(value, ("group", "dev"), split_axis=0, concat_axis=0, tiled=True)
        return value.reshape(total * 2 * cap, width // 2)

    held = {wrap(OWN): passages}

    def source(to, step):
        return wrap((to[0] - step[0], to[1] - step[1]))

    def spread(stage, *others):
        names = [source(to, step) for to, step in stage]
        values = tie([held[n] for n in names], *others) if others else [held[n] for n in names]
        for (to, step), value in zip(stage, values):
            held[wrap(to)] = shift(value, step)

    def round_of(number):
        return [held[wrap(to)] for to, _ in ROUNDS[number]]

    spread(ROUNDS[0])
    owners = mined_owner[:, 0].reshape(total, -1)
    names = mined_row.reshape(total, -1)
    outgoing, hot, pick = serve(me.astype(I32).reshape(1, 1), owners, names, passages, cap)
    arrived = exchange(outgoing)
    blocks = lambda chunk: [held[wrap(o)] for o in chunk]
    spread(ROUNDS[1], owners, names, round_of(0))
    spread(ROUNDS[2], round_of(1), round_of(0))
    near = CHUNKS[0] + CHUNKS[1]
    e1, stat1 = logits(near, at, pa, pb, queries, other, blocks(near), None)
    spread(ROUNDS[3], stat1, round_of(2))
    mined, e_mined, stat_mined = mined_logits(arrived, pick, queries, stat1, cap)
    far = CHUNKS[2] + CHUNKS[3]
    e2, stat = logits(far, at, pa, pb, queries, other, blocks(far), stat_mined)
    there = swap(stat)

    grads = {}

    def collect(number, g, *stamps):
        chunk, stage = CHUNKS[number], ROUNDS[number]
        n = passages.shape[0]
        for b, o in enumerate(chunk):
            grads.setdefault(wrap(o), []).insert(0, g[b * n : (b + 1) * n])
        zeros = [stamp[0, 0].astype(F32) * 0.0 for stamp in stamps]
        arrived = []
        for to, step in stage:
            send = functools.reduce(jnp.add, [v.astype(F32) for v in grads[wrap(to)]] + zeros).astype(LINK)
            arrived.append(shift(send, (-step[0], -step[1])))
            grads.setdefault(source(to, step), []).append(arrived[-1])
        return arrived

    groups_of = (near, far)
    (g1, g2), own, theirs, w_done = weights(
        groups_of, at, pa, pb, stat, there, (stat1, stat), (e1, e2), queries, other, blocks(near + far)
    )
    split = len(CHUNKS[0]) * passages.shape[0]
    arrived = collect(3, g2[split:])
    theirs = swap(theirs)
    w_mined, back, losses, mined_done = mined_weights(stat, there, stat_mined, e_mined, queries, pick, cap, w_done)
    returned = exchange(back)
    collect(2, g2[:split], mined_done, arrived[1], arrived[3])
    mine, mine_done = finish(own, theirs, w_mined, mined)
    collect(1, g1[split:], mine_done)
    collect(0, g1[:split])
    owned = owned_sum(hot, returned, cap)
    passage = functools.reduce(jnp.add, [v.astype(F32) for v in grads[wrap(OWN)]] + [owned])
    return losses.reshape(rows), mine, passage


def solution(mesh):
    placed = (P(("group", "dev"), None), P(("group", "dev"), None), P(), P(), P(("group", "dev")))
    return jax.shard_map(
        local,
        mesh=mesh,
        in_specs=placed,
        out_specs=(P(("group", "dev")), P(("group", "dev"), None), P(("group", "dev"), None)),
        check_vma=False,
    )
```
